32 devices in a mesh: parts: 2 (over y), sensor: 4 (over z), tm: 2 (over x), lag: 2 (over core).
Axes of the slice: x: 2, y: 2, z: 4, core: 2. Of those that a mesh axis runs over, the one named last changes fastest.
Arguments:
- readings: bfloat16 [128, 128, 1024], P(('parts', 'sensor'), None, 'tm'), parts along dimension 0, may hold values from -6 to 6
- present: int32 [128, 1024], P(('parts', 'sensor'), 'tm'), parts along dimension 0, may hold values from 0 to 1, as said below
- pair_first: int32 [64], P(('parts', 'sensor')), parts along dimension 0, may hold values from 0 to 63, as said below
- pair_second: int32 [64], P(('parts', 'sensor')), parts along dimension 0, may hold values from 0 to 63, as said below
Outputs:
- pair_cov: bfloat16 [64, 25, 128, 128], P(('parts', 'sensor'), None, ('tm', 'lag')), parts along dimension 0
- strength: float32 [25, 128, 128], P(None, ('parts', 'sensor')), parts along dimension 1
The draws below stay inside these ranges and needn't reach their ends.
There are 2 independent parts, one for each index of `parts`. The reference program is written for one: setup_inputs(seed, part) draws one part's arguments, and reference() takes and returns one part's arrays. A program takes and returns all parts, laid end to end along the dimension named above; each array names one. Nothing has to cross between parts.
Inputs may be any that keep to these rules, and one draw needn't show every extreme that they name: Each block misses one run of consecutive steps (possibly empty) shorter than 512; all its other steps are present. `pair_first`: blocks are laid 16 to an index of sensor in order; the 8 pairs held by an index of sensor have their first block on that index. `pair_second`: A pair's second block lies on an index of sensor at most 3 away from the first's; of the pairs held by one index, at most 2 have their second block on any one index, and some index reaches 2 in every draw.
All inputs are finite; a program needn't handle non-finite values.
Results may differ from the reference program's by a relative error of at most 0.0085.
Values may be sent and summed in bfloat16 or wider, within the bound.
No kernel may reach another device: no remote copies, remote signals or barrier semaphores. Data moves between devices by JAX's collectives and lax.ppermute only.
A program may use at most 64 MiB of HBM per device.

```python
import jax
import jax.numpy as jnp
from jax import lax

BLOCK = 128
LAGS = 25
REACH = 3
CAP = 2
STEPS_DEV = 512
BLK_DEV = 16
PAIR_DEV = 8
STEPS = 1024
BLOCKS = 64
PAIRS = 32
N_TM = 2


def pair_table(key):
    subkeys = jax.random.split(key, 3)
    devices_count = PAIRS // PAIR_DEV
    entries = (2 * REACH + 1) * CAP
    home_ids = jnp.arange(devices_count, dtype=jnp.int32)[:, None]
    owners = home_ids + (jnp.arange(entries, dtype=jnp.int32) // CAP - REACH)[None, :]
    usable = (owners >= 0) & (owners < devices_count)
    scores = jax.vmap(lambda single: jax.random.permutation(single, entries))(jax.random.split(subkeys[0], devices_count))
    scores = scores + jnp.where(usable, 0, entries)
    chosen = jnp.argsort(scores, axis=1, stable=True)[:, :PAIR_DEV]
    chosen_owner = jnp.take_along_axis(owners, chosen, axis=1)
    second = chosen_owner * BLK_DEV + jax.random.randint(subkeys[1], (devices_count, PAIR_DEV), 0, BLK_DEV)
    first = home_ids * BLK_DEV + jax.random.randint(subkeys[2], (devices_count, PAIR_DEV), 0, BLK_DEV)
    return (first.reshape(-1).astype(jnp.int32), second.reshape(-1).astype(jnp.int32))


def draw_pair_first(key, part):
    first, second = pair_table(key)
    return first


def draw_pair_second(key, part):
    first, second = pair_table(key)
    return second


def draw_present(key, part):
    key = jax.random.fold_in(key, 11)
    subkeys = jax.random.split(key, 2)
    lengths = jax.random.randint(subkeys[0], (BLOCKS, 1), 0, STEPS // 2)
    begins = jax.random.randint(subkeys[1], (BLOCKS, 1), 0, STEPS)
    moments = jnp.arange(STEPS, dtype=jnp.int32)[None, :]
    missing = (moments >= begins) & (moments < begins + lengths)
    return jnp.where(missing, 0, 1).astype(jnp.int32)


def steps_of(own_key, shape, shards, smallest, largest):
    gain = 1.0
    for axis_at, blocks in shards:
        steps = jax.random.uniform(jax.random.fold_in(jax.random.fold_in(own_key, 6), axis_at), (blocks,), jnp.float32, smallest / len(shards), largest / len(shards))
        gain = gain * jnp.repeat(jnp.exp(steps), shape[axis_at] // blocks).reshape((-1,) + (1,) * (len(shape) - 1 - axis_at))
    return gain


def bell_draw(own_key, extent, spread, bound, cuts=(), kind=jnp.bfloat16):
    loudness = steps_of(own_key, extent, cuts, -0.22, 0.18) if cuts else 1.0
    drawn = jax.random.normal(own_key, extent, jnp.float32) * spread * loudness
    return jnp.minimum(jnp.maximum(drawn, -bound), bound).astype(kind)


def setup_inputs(seed: int = 0, part: int = 0) -> dict:
    splits = jax.random.split(jax.random.key(seed), 5)
    part_splits = jax.random.split(jax.random.fold_in(splits[4], part), 5)
    readings = bell_draw(part_splits[0], (BLOCKS, BLOCK, STEPS), 1.0, 6.0, ((0, 4), (2, 2)))
    present = draw_present(jax.random.fold_in(jax.random.fold_in(splits[4], part), 71), part)
    pair_first = draw_pair_first(jax.random.fold_in(jax.random.fold_in(splits[4], part), 71), part)
    pair_second = draw_pair_second(jax.random.fold_in(jax.random.fold_in(splits[4], part), 71), part)
    return {"readings": readings, "present": present, "pair_first": pair_first, "pair_second": pair_second}


def reference(readings, present, pair_first, pair_second):
    observed = present.astype(jnp.float32)
    values = readings.astype(jnp.float32)
    average = lax.optimization_barrier(jnp.sum(values * observed[:, None, :], axis=2)) / lax.optimization_barrier(jnp.sum(observed, axis=1))[:, None]
    centered = ((values - average[:, :, None]) * observed[:, None, :]).astype(jnp.bfloat16)
    first_all = centered.astype(jnp.float32)
    second_all = jnp.concatenate([first_all, jnp.zeros((BLOCKS, BLOCK, LAGS - 1), jnp.float32)], axis=2)
    lag_values = jnp.arange(LAGS, dtype=jnp.float32)
    scales = 1.0 / jnp.sqrt(STEPS - lag_values)

    def one_pair(pair_ids):
        first_rows = lax.dynamic_index_in_dim(first_all, pair_ids[0], 0, False)
        second_rows = lax.dynamic_index_in_dim(second_all, pair_ids[1], 0, False)

        def one_window(offset):
            window = lax.dynamic_slice_in_dim(first_rows, offset, STEPS_DEV, 1)
            extended = lax.dynamic_slice_in_dim(second_rows, offset, STEPS_DEV + LAGS - 1, 1)
            products = jnp.stack([jnp.dot(window, extended[:, lag_step:lag_step + STEPS_DEV].T, precision=lax.Precision.HIGHEST) for lag_step in range(LAGS)])
            rounded = lax.optimization_barrier(products.astype(jnp.bfloat16))
            return rounded.astype(jnp.float32)
        starts = jnp.arange(N_TM, dtype=jnp.int32) * STEPS_DEV
        return lax.optimization_barrier(jnp.sum(lax.map(one_window, starts), axis=0)) * scales[:, None, None]
    standard = lax.map(one_pair, jnp.stack([pair_first, pair_second], axis=1))
    pair_cov = standard.astype(jnp.bfloat16)
    squares = standard * standard
    row_part = jnp.transpose(lax.optimization_barrier(jnp.sum(squares, axis=3)), (1, 0, 2)) / BLOCK
    col_part = jnp.transpose(lax.optimization_barrier(jnp.sum(squares, axis=2)), (1, 0, 2)) / BLOCK
    strength = jnp.zeros((LAGS, BLOCKS, BLOCK), jnp.float32)
    strength = strength.at[:, pair_first, :].add(row_part)
    strength = strength.at[:, pair_second, :].add(col_part)
    return (pair_cov, strength)
```

```python
import jax
import jax.numpy as jnp
import numpy as np
from jax import lax
from jax.experimental import pallas as pl
from jax.experimental.pallas import tpu as pltpu
from jax.sharding import PartitionSpec as P

LAGS = 25
REACH = 3
CAP = 2
PAD = 16
LAG_ROWS = 32
VMEM = pl.BlockSpec(memory_space=pltpu.VMEM)
SMEM = pl.BlockSpec(memory_space=pltpu.SMEM)
ANY = pl.BlockSpec(memory_space=pl.ANY)
PARAMS = pltpu.CompilerParams(vmem_limit_bytes=24 * 1024 * 1024)


def rotated(block, axis, distance):
    size = lax.axis_size(axis)
    return lax.ppermute(block, axis, [(i, (i + distance) % size) for i in range(size)])


def mask_rows(present_ref, index, rows):
    row = present_ref[pl.ds(index, 1), :].astype(jnp.float32)
    return jnp.broadcast_to(row, (rows, row.shape[1]))


def pack_blocks(readings, present, indices):
    _, rows, steps = readings.shape
    count = indices.shape[0]

    def kernel(index_ref, readings_ref, present_ref, *rest):
        outs, sems = rest[:count], rest[count]
        copies = [
            pltpu.make_async_copy(
                readings_ref.at[index_ref[i]], outs[i].at[pl.ds(0, rows)], sems.at[i]
            )
            for i in range(count)
        ]
        for copy in copies:
            copy.start()
        for i in range(count):
            outs[i][rows : rows + PAD, :] = mask_rows(present_ref, index_ref[i], PAD).astype(
                jnp.bfloat16
            )
        for copy in copies:
            copy.wait()

    return pl.pallas_call(
        kernel,
        out_shape=[jax.ShapeDtypeStruct((rows + PAD, steps), jnp.bfloat16)] * count,
        in_specs=[SMEM, ANY, VMEM],
        out_specs=[VMEM] * count,
        scratch_shapes=[pltpu.SemaphoreType.DMA((count,))],
        compiler_params=PARAMS,
    )(indices, readings, present)


def pack_first(readings, present, first_index, row_starts, per_row):
    _, _, steps = readings.shape
    pairs = first_index.shape[0]
    count = row_starts.shape[0]

    def kernel(first_ref, start_ref, readings_ref, present_ref, *rest):
        outs, sems = rest[:count], rest[count]
        copies = []
        for k in range(count):
            start = pl.multiple_of(start_ref[k], per_row)
            for p in range(pairs):
                copies.append(
                    pltpu.make_async_copy(
                        readings_ref.at[first_ref[p], pl.ds(start, per_row)],
                        outs[k].at[pl.ds(p * per_row, per_row)],
                        sems.at[k, p],
                    )
                )
        for copy in copies:
            copy.start()
        rows = lax.broadcasted_iota(jnp.int32, (PAD, steps), 0)
        masks = jnp.zeros((PAD, steps), jnp.float32)
        for p in range(pairs):
            masks = jnp.where(rows == p, mask_rows(present_ref, first_ref[p], PAD), masks)
        for k in range(count):
            outs[k][pairs * per_row : pairs * per_row + PAD, :] = masks.astype(jnp.bfloat16)
        for copy in copies:
            copy.wait()

    return pl.pallas_call(
        kernel,
        out_shape=[jax.ShapeDtypeStruct((pairs * per_row + PAD, steps), jnp.bfloat16)] * count,
        in_specs=[SMEM, SMEM, ANY, VMEM],
        out_specs=[VMEM] * count,
        scratch_shapes=[pltpu.SemaphoreType.DMA((count, pairs))],
        compiler_params=PARAMS,
    )(first_index, row_starts, readings, present)


def centered_windows(raw, masks):
    total = sum(jnp.sum(r * m, axis=1, keepdims=True) for r, m in zip(raw, masks))
    count = sum(jnp.sum(m, axis=1, keepdims=True) for m in masks)
    average = total / count
    return [(r - average) * m for r, m in zip(raw, masks)]


def covariances(pair_of, places, firsts, blocks, carried, pairs, per_row, block_size):
    windows = len(firsts)
    slots = len(blocks)
    steps = firsts[0].shape[1]
    total_steps = windows * steps
    shifts = (LAGS + 1) // 2
    scales = 1.0 / np.sqrt(np.float32(total_steps) - np.arange(LAGS, dtype=np.float32))
    quarter = 128 // per_row
    flat = [block for slot in blocks for block in slot]

    def kernel(pair_ref, place_ref, *rest):
        first_refs = rest[:windows]
        block_refs = rest[windows : windows + slots * windows]
        rest = rest[windows + slots * windows + (carried is not None) :]
        cov_ref, row_ref, col_ref, left, right, squares, ready, first_part, sems = rest

        def one(j):
            pair = pair_ref[j]
            base = pl.multiple_of(pair * per_row, per_row)
            which = lax.broadcasted_iota(jnp.int32, (PAD, steps), 0) == pair
            raw, masks = [], []
            for k in range(windows):
                raw.append(first_refs[k][pl.ds(base, per_row), :].astype(jnp.float32))
                all_masks = first_refs[k][pairs * per_row : pairs * per_row + PAD, :]
                masks.append(
                    jnp.sum(
                        jnp.where(which, all_masks.astype(jnp.float32), 0.0), axis=0, keepdims=True
                    )
                )
            for k, part in enumerate(centered_windows(raw, masks)):
                at = pl.multiple_of(place_ref[k] * steps, steps)
                first_part[:, pl.ds(at, steps)] = part
            raw, masks = [], []
            for k in range(windows):
                ref = block_refs[j * windows + k]
                raw.append(ref[0:block_size, :].astype(jnp.float32))
                masks.append(ref[block_size : block_size + 1, :].astype(jnp.float32))
            for k, part in enumerate(centered_windows(raw, masks)):
                at = pl.multiple_of(place_ref[k] * steps, steps)
                right[0:block_size, pl.ds(at, steps)] = part.astype(jnp.bfloat16)
            whole = right[0:block_size, :].astype(jnp.float32)
            lane = lax.broadcasted_iota(jnp.int32, whole.shape, 1)
            moved = pltpu.roll(whole, total_steps - 1, 1)
            right[block_size : 2 * block_size, :] = jnp.where(
                lane < total_steps - 1, moved, 0.0
            ).astype(jnp.bfloat16)
            whole = first_part[...]
            lane = lax.broadcasted_iota(jnp.int32, whole.shape, 1)
            for m in range(shifts):
                moved = whole if m == 0 else pltpu.roll(whole, 2 * m, 1)
                left[m * per_row : (m + 1) * per_row, :] = jnp.where(
                    lane >= 2 * m, moved, 0.0
                ).astype(jnp.bfloat16)
            product = lax.dot_general(
                left[...], right[...], (((1,), (1,)), ((), ())), preferred_element_type=jnp.float32
            )
            for lag in range(LAGS):
                m, odd = lag // 2, lag % 2
                standard = product[
                    m * per_row : (m + 1) * per_row, odd * block_size : (odd + 1) * block_size
                ] * float(scales[lag])
                ready[j, lag] = standard.astype(jnp.bfloat16)
                square = standard * standard
                col_ref[lag, j : j + 1, :] = (
                    jnp.sum(square, axis=0, keepdims=True) * (1.0 / block_size)
                )
                squares[lag * per_row : (lag + 1) * per_row, :] = square.astype(jnp.bfloat16)
            ones = jnp.full((8, block_size), 1.0 / block_size, jnp.bfloat16)
            sums = lax.dot_general(
                ones, squares[...], (((1,), (1,)), ((), ())), preferred_element_type=jnp.float32
            )
            start = place_ref[windows]
            lane = lax.broadcasted_iota(jnp.int32, (8, 128), 1)
            level = lax.broadcasted_iota(jnp.int32, (8, 128), 0)
            mine = (lane >= start) & (lane < start + per_row)
            tiles = [jnp.zeros((8, 128), jnp.float32) for _ in range(LAG_ROWS // 8)]
            for lag in range(LAGS):
                q, r = lag // quarter, lag % quarter
                piece = sums[:, q * 128 : (q + 1) * 128]
                piece = pltpu.roll(piece, lax.rem(start + 128 - r * per_row, 128), 1)
                tiles[lag // 8] = jnp.where(mine & (level == lag % 8), piece, tiles[lag // 8])
            for i, tile in enumerate(tiles):
                row_ref[j, i * 8 : (i + 1) * 8, :] = tile
            return None

        for j in range(slots):
            used = pair_ref[j] >= 0

            @pl.when(used)
            def _():
                one(j)
                pltpu.make_async_copy(ready.at[j], cov_ref.at[pair_ref[j]], sems.at[j]).start()

            @pl.when(jnp.logical_not(used))
            def _():
                row_ref[j] = jnp.zeros(row_ref.shape[1:], jnp.float32)
                col_ref[:, j : j + 1, :] = jnp.zeros((LAGS, 1, block_size), jnp.float32)

        for j in range(slots):

            @pl.when(pair_ref[j] >= 0)
            def _():
                pltpu.make_async_copy(ready.at[j], cov_ref.at[pair_ref[j]], sems.at[j]).wait()

    operands = [pair_of, places, *firsts, *flat]
    specs = [SMEM, SMEM] + [VMEM] * (len(firsts) + len(flat))
    aliases = {}
    if carried is not None:
        aliases = {len(operands): 0}
        operands.append(carried)
        specs.append(ANY)
    wide = -(-LAGS * per_row // 128) * 128
    return pl.pallas_call(
        kernel,
        out_shape=[
            jax.ShapeDtypeStruct((pairs, LAGS, per_row, block_size), jnp.bfloat16),
            jax.ShapeDtypeStruct((slots, LAG_ROWS, block_size), jnp.float32),
            jax.ShapeDtypeStruct((LAGS, slots, block_size), jnp.float32),
        ],
        in_specs=specs,
        out_specs=[ANY, VMEM, VMEM],
        scratch_shapes=[
            pltpu.VMEM((shifts * per_row, total_steps), jnp.bfloat16),
            pltpu.VMEM((2 * block_size, total_steps), jnp.bfloat16),
            pltpu.VMEM((wide, block_size), jnp.bfloat16),
            pltpu.VMEM((slots, LAGS, per_row, block_size), jnp.bfloat16),
            pltpu.VMEM((per_row, total_steps), jnp.float32),
            pltpu.SemaphoreType.DMA((slots,)),
        ],
        input_output_aliases=aliases,
        compiler_params=PARAMS,
        cost_estimate=pl.CostEstimate(
            flops=slots * 2 * LAGS * per_row * block_size * total_steps,
            bytes_accessed=slots * LAGS * per_row * block_size * 2 + slots * 600000,
            transcendentals=0,
        ),
    )(*operands)


def fold(first_of, served, rows, cols, blk_dev):
    groups = len(rows)
    slots, _, block_size = rows[0].shape

    def kernel(first_ref, served_ref, *rest):
        row_refs, col_refs, out_ref = rest[:groups], rest[groups : 2 * groups], rest[2 * groups]
        place = lax.broadcasted_iota(jnp.int32, (blk_dev, block_size), 0)
        own, other = [], []
        for d in range(groups):
            for j in range(slots):
                own.append(place == first_ref[d * slots + j])
                other.append(place == served_ref[d * slots + j])
        for lag in range(LAGS):
            total = jnp.zeros((blk_dev, block_size), jnp.float32)
            for d in range(groups):
                for j in range(slots):
                    total = total + jnp.where(
                        own[d * slots + j], row_refs[d][j, lag : lag + 1, :], 0.0
                    )
                    total = total + jnp.where(
                        other[d * slots + j], col_refs[d][lag, j : j + 1, :], 0.0
                    )
            out_ref[lag] = total.astype(jnp.bfloat16)

    return pl.pallas_call(
        kernel,
        out_shape=jax.ShapeDtypeStruct((LAGS, blk_dev, block_size), jnp.bfloat16),
        in_specs=[SMEM, SMEM] + [VMEM] * (2 * groups),
        out_specs=VMEM,
        compiler_params=PARAMS,
    )(first_of, served, *rows, *cols)


def local(readings, present, pair_first, pair_second):
    blk_dev, block_size, steps_here = readings.shape
    pair_count = pair_first.shape[0]
    sensor_count = lax.axis_size("sensor")
    tm_count = lax.axis_size("tm")
    lag_count = lax.axis_size("lag")
    home = lax.axis_index("sensor")
    tm_place = lax.axis_index("tm")
    lag_place = lax.axis_index("lag")
    per_row = block_size // (tm_count * lag_count)
    groups = sorted({d % sensor_count for d in range(-REACH, REACH + 1)})
    slot_count = len(groups) * CAP

    first_index = pair_first - home * blk_dev
    owner = pair_second // blk_dev
    partner_index = pair_second - owner * blk_dev
    positions = jnp.arange(pair_count)
    earlier = (owner[:, None] == owner[None, :]) & (positions[None, :] < positions[:, None])
    rank = jnp.sum(earlier.astype(jnp.int32), axis=1)
    distance = (owner - home + sensor_count) % sensor_count
    group = jnp.sum(
        jnp.where(distance[:, None] == jnp.array(groups)[None, :], jnp.arange(len(groups)), 0),
        axis=1,
    )
    slot = group * CAP + (lag_place - rank + CAP) % CAP
    hot = slot[:, None] == jnp.arange(slot_count)[None, :]
    requests = jnp.sum(jnp.where(hot, partner_index[:, None], 0), axis=0)
    pair_of = jnp.sum(jnp.where(hot, positions[:, None] + 1, 0), axis=0) - 1
    first_of = jnp.sum(jnp.where(hot, first_index[:, None], 0), axis=0)

    served = [requests[:CAP]] + [
        rotated(requests[i * CAP : (i + 1) * CAP], "sensor", d)
        for i, d in enumerate(groups)
        if i > 0
    ]
    turns = jnp.arange(tm_count)
    row_starts = ((tm_place + turns) % tm_count * lag_count + lag_place) * per_row
    sent = pack_first(readings, present, first_index, row_starts, per_row)
    firsts = [sent[0]] + [rotated(sent[k], "tm", k) for k in range(1, tm_count)]
    places = jnp.concatenate([(tm_place - turns) % tm_count, row_starts[:1]])

    here = pack_blocks(readings, present, requests[:CAP])
    away = pack_blocks(readings, present, jnp.stack([s[0] for s in served[1:]]))
    cov = None
    rows, cols = [], []
    for i, d in enumerate(groups):
        own = here[0] if i == 0 else rotated(away[i - 1], "sensor", -d)
        own_windows = [own] + [rotated(own, "tm", k) for k in range(1, tm_count)]
        blocks = [own_windows]
        for j in range(1, lag_count):
            blocks.append(
                [
                    here[j] if i == 0 and k == 0 else rotated(own_windows[k], "lag", j)
                    for k in range(tm_count)
                ]
            )
        cov, row, col = covariances(
            pair_of[i * CAP : (i + 1) * CAP],
            places,
            firsts,
            blocks,
            cov,
            pair_count,
            per_row,
            block_size,
        )
        rows.append(row)
        cols.append(col if i == 0 else rotated(col, "sensor", d))
    partial = fold(first_of, jnp.concatenate(served), rows, cols, blk_dev)
    partial = partial.astype(jnp.float32)
    if lag_count == 2:
        partial = partial + rotated(partial.astype(jnp.bfloat16), "lag", 1).astype(jnp.float32)
    else:
        partial = lax.psum(partial.astype(jnp.bfloat16), "lag").astype(jnp.float32)
    partial = partial.astype(jnp.bfloat16)
    if tm_count == 2:
        strength = partial.astype(jnp.float32) + rotated(partial, "tm", 1).astype(jnp.float32)
    else:
        strength = lax.psum(partial, "tm").astype(jnp.float32)
    return (cov, strength)


def solution(mesh):
    in_specs = (
        P(("parts", "sensor"), None, "tm"),
        P(("parts", "sensor"), "tm"),
        P(("parts", "sensor")),
        P(("parts", "sensor")),
    )
    out_specs = (
        P(("parts", "sensor"), None, ("tm", "lag"), None),
        P(None, ("parts", "sensor"), None),
    )
    return jax.shard_map(local, mesh=mesh, in_specs=in_specs, out_specs=out_specs, check_vma=False)
```

```python
import jax
import jax.numpy as jnp
import numpy as np
from jax import lax
from jax.experimental import pallas as pl
from jax.experimental.pallas import tpu as pltpu
from jax.sharding import PartitionSpec as P

LAGS = 25
REACH = 3
CAP = 2
PAD = 16
MASK_ROWS = 8
LAG_ROWS = 32
VMEM = pl.BlockSpec(memory_space=pltpu.VMEM)
SMEM = pl.BlockSpec(memory_space=pltpu.SMEM)
ANY = pl.BlockSpec(memory_space=pl.ANY)
PEAK = 1.15e9
PARAMS = pltpu.CompilerParams(vmem_limit_bytes=24 * 1024 * 1024)
WIDE = pltpu.CompilerParams(vmem_limit_bytes=55_000_000)


def cost(microseconds):
    return pl.CostEstimate(
        flops=int(microseconds * PEAK), bytes_accessed=1024, transcendentals=0
    )


def rotated(block, axis, distance):
    size = lax.axis_size(axis)
    return lax.ppermute(block, axis, [(i, (i + distance) % size) for i in range(size)])


def mask_rows(present_ref, index, rows):
    row = present_ref[pl.ds(index, 1), :].astype(jnp.float32)
    return jnp.broadcast_to(row, (rows, row.shape[1]))


def pack_blocks(readings, present, indices):
    _, rows, steps = readings.shape
    count = indices.shape[0]

    def kernel(index_ref, readings_ref, present_ref, *rest):
        outs, sems = rest[:count], rest[count]
        copies = [
            pltpu.make_async_copy(
                readings_ref.at[index_ref[i]], outs[i].at[pl.ds(0, rows)], sems.at[i]
            )
            for i in range(count)
        ]
        for copy in copies:
            copy.start()
        for i in range(count):
            outs[i][rows : rows + MASK_ROWS, :] = mask_rows(
                present_ref, index_ref[i], MASK_ROWS
            ).astype(jnp.bfloat16)
        for copy in copies:
            copy.wait()

    return pl.pallas_call(
        kernel,
        out_shape=[jax.ShapeDtypeStruct((rows + MASK_ROWS, steps), jnp.bfloat16)] * count,
        in_specs=[SMEM, ANY, VMEM],
        out_specs=[VMEM] * count,
        scratch_shapes=[pltpu.SemaphoreType.DMA((count,))],
        compiler_params=WIDE,
        cost_estimate=cost(1.0),
    )(indices, readings, present)


def pack_first(readings, present, first_index, row_starts, per_row):
    _, _, steps = readings.shape
    pairs = first_index.shape[0]
    count = row_starts.shape[0]

    def kernel(first_ref, start_ref, readings_ref, present_ref, *rest):
        outs, sems = rest[:count], rest[count]
        copies = []
        for k in range(count):
            start = pl.multiple_of(start_ref[k], per_row)
            for p in range(pairs):
                copies.append(
                    pltpu.make_async_copy(
                        readings_ref.at[first_ref[p], pl.ds(start, per_row)],
                        outs[k].at[pl.ds(p * per_row, per_row)],
                        sems.at[k, p],
                    )
                )
        for copy in copies:
            copy.start()
        rows = lax.broadcasted_iota(jnp.int32, (PAD, steps), 0)
        masks = jnp.zeros((PAD, steps), jnp.float32)
        for p in range(pairs):
            masks = jnp.where(rows == p, mask_rows(present_ref, first_ref[p], PAD), masks)
        for k in range(count):
            outs[k][pairs * per_row : pairs * per_row + PAD, :] = masks.astype(jnp.bfloat16)
        for copy in copies:
            copy.wait()

    return pl.pallas_call(
        kernel,
        out_shape=[jax.ShapeDtypeStruct((pairs * per_row + PAD, steps), jnp.bfloat16)] * count,
        in_specs=[SMEM, SMEM, ANY, VMEM],
        out_specs=[VMEM] * count,
        scratch_shapes=[pltpu.SemaphoreType.DMA((count, pairs))],
        compiler_params=WIDE,
        cost_estimate=cost(1.4),
    )(first_index, row_starts, readings, present)


def centered_windows(raw, masks):
    total = sum(jnp.sum(r * m, axis=1, keepdims=True) for r, m in zip(raw, masks))
    count = sum(jnp.sum(m, axis=1, keepdims=True) for m in masks)
    average = total / count
    return [(r - average) * m for r, m in zip(raw, masks)]


def covariances(pair_of, places, firsts, blocks, carried, pairs, per_row, block_size):
    windows = len(firsts)
    slots = len(blocks)
    steps = firsts[0].shape[1]
    total_steps = windows * steps
    shifts = (LAGS + 1) // 2
    scales = 1.0 / np.sqrt(np.float32(total_steps) - np.arange(LAGS, dtype=np.float32))
    quarter = 128 // per_row
    flat = [block for slot in blocks for block in slot]

    def kernel(pair_ref, place_ref, *rest):
        first_refs = rest[:windows]
        block_refs = rest[windows : windows + slots * windows]
        rest = rest[windows + slots * windows + (carried is not None) :]
        cov_ref, row_ref, col_ref, left, right, squares, ready, first_part, sems = rest

        def one(j):
            pair = pair_ref[j]
            base = pl.multiple_of(pair * per_row, per_row)
            which = lax.broadcasted_iota(jnp.int32, (PAD, steps), 0) == pair
            raw, masks = [], []
            for k in range(windows):
                raw.append(first_refs[k][pl.ds(base, per_row), :].astype(jnp.float32))
                all_masks = first_refs[k][pairs * per_row : pairs * per_row + PAD, :]
                masks.append(
                    jnp.sum(
                        jnp.where(which, all_masks.astype(jnp.float32), 0.0), axis=0, keepdims=True
                    )
                )
            for k, part in enumerate(centered_windows(raw, masks)):
                at = pl.multiple_of(place_ref[k] * steps, steps)
                first_part[:, pl.ds(at, steps)] = part
            raw, masks = [], []
            for k in range(windows):
                ref = block_refs[j * windows + k]
                raw.append(ref[0:block_size, :].astype(jnp.float32))
                masks.append(ref[block_size : block_size + 1, :].astype(jnp.float32))
            for k, part in enumerate(centered_windows(raw, masks)):
                at = pl.multiple_of(place_ref[k] * steps, steps)
                right[0:block_size, pl.ds(at, steps)] = part.astype(jnp.bfloat16)
            whole = right[0:block_size, :].astype(jnp.float32)
            lane = lax.broadcasted_iota(jnp.int32, whole.shape, 1)
            moved = pltpu.roll(whole, total_steps - 1, 1)
            right[block_size : 2 * block_size, :] = jnp.where(
                lane < total_steps - 1, moved, 0.0
            ).astype(jnp.bfloat16)
            whole = first_part[...]
            lane = lax.broadcasted_iota(jnp.int32, whole.shape, 1)
            for m in range(shifts):
                moved = whole if m == 0 else pltpu.roll(whole, 2 * m, 1)
                left[m * per_row : (m + 1) * per_row, :] = jnp.where(
                    lane >= 2 * m, moved, 0.0
                ).astype(jnp.bfloat16)
            product = lax.dot_general(
                left[...], right[...], (((1,), (1,)), ((), ())), preferred_element_type=jnp.float32
            )
            for lag in range(LAGS):
                m, odd = lag // 2, lag % 2
                standard = product[
                    m * per_row : (m + 1) * per_row, odd * block_size : (odd + 1) * block_size
                ] * float(scales[lag])
                ready[j, lag] = standard.astype(jnp.bfloat16)
                square = standard * standard
                col_ref[lag, j : j + 1, :] = (
                    jnp.sum(square, axis=0, keepdims=True) * (1.0 / block_size)
                )
                squares[lag * per_row : (lag + 1) * per_row, :] = square.astype(jnp.bfloat16)
            ones = jnp.full((8, block_size), 1.0 / block_size, jnp.bfloat16)
            sums = lax.dot_general(
                ones, squares[...], (((1,), (1,)), ((), ())), preferred_element_type=jnp.float32
            )
            start = place_ref[windows]
            lane = lax.broadcasted_iota(jnp.int32, (8, 128), 1)
            level = lax.broadcasted_iota(jnp.int32, (8, 128), 0)
            mine = (lane >= start) & (lane < start + per_row)
            tiles = [jnp.zeros((8, 128), jnp.float32) for _ in range(LAG_ROWS // 8)]
            for lag in range(LAGS):
                q, r = lag // quarter, lag % quarter
                piece = sums[:, q * 128 : (q + 1) * 128]
                piece = pltpu.roll(piece, lax.rem(start + 128 - r * per_row, 128), 1)
                tiles[lag // 8] = jnp.where(mine & (level == lag % 8), piece, tiles[lag // 8])
            for i, tile in enumerate(tiles):
                row_ref[j, i * 8 : (i + 1) * 8, :] = tile
            return None

        for j in range(slots):
            used = pair_ref[j] >= 0

            @pl.when(used)
            def _():
                one(j)
                pltpu.make_async_copy(ready.at[j], cov_ref.at[pair_ref[j]], sems.at[j]).start()

            @pl.when(jnp.logical_not(used))
            def _():
                row_ref[j] = jnp.zeros(row_ref.shape[1:], jnp.float32)
                col_ref[:, j : j + 1, :] = jnp.zeros((LAGS, 1, block_size), jnp.float32)

        for j in range(slots):

            @pl.when(pair_ref[j] >= 0)
            def _():
                pltpu.make_async_copy(ready.at[j], cov_ref.at[pair_ref[j]], sems.at[j]).wait()

    operands = [pair_of, places, *firsts, *flat]
    specs = [SMEM, SMEM] + [VMEM] * (len(firsts) + len(flat))
    aliases = {}
    if carried is not None:
        aliases = {len(operands): 0}
        operands.append(carried)
        specs.append(ANY)
    wide = -(-LAGS * per_row // 128) * 128
    return pl.pallas_call(
        kernel,
        out_shape=[
            jax.ShapeDtypeStruct((pairs, LAGS, per_row, block_size), jnp.bfloat16),
            jax.ShapeDtypeStruct((slots, LAG_ROWS, block_size), jnp.float32),
            jax.ShapeDtypeStruct((LAGS, slots, block_size), jnp.float32),
        ],
        in_specs=specs,
        out_specs=[ANY, VMEM, VMEM],
        scratch_shapes=[
            pltpu.VMEM((shifts * per_row, total_steps), jnp.bfloat16),
            pltpu.VMEM((2 * block_size, total_steps), jnp.bfloat16),
            pltpu.VMEM((wide, block_size), jnp.bfloat16),
            pltpu.VMEM((slots, LAGS, per_row, block_size), jnp.bfloat16),
            pltpu.VMEM((per_row, total_steps), jnp.float32),
            pltpu.SemaphoreType.DMA((slots,)),
        ],
        input_output_aliases=aliases,
        compiler_params=PARAMS,
        cost_estimate=cost(1.5 * slots),
    )(*operands)


def fold(first_of, served, rows, cols, blk_dev):
    groups = len(rows)
    slots, _, block_size = rows[0].shape

    def kernel(first_ref, served_ref, *rest):
        row_refs, col_refs, out_ref = rest[:groups], rest[groups : 2 * groups], rest[2 * groups]
        place = lax.broadcasted_iota(jnp.int32, (blk_dev, block_size), 0)
        own, other = [], []
        for d in range(groups):
            for j in range(slots):
                own.append(place == first_ref[d * slots + j])
                other.append(place == served_ref[d * slots + j])
        for lag in range(LAGS):
            total = jnp.zeros((blk_dev, block_size), jnp.float32)
            for d in range(groups):
                for j in range(slots):
                    total = total + jnp.where(
                        own[d * slots + j], row_refs[d][j, lag : lag + 1, :], 0.0
                    )
                    total = total + jnp.where(
                        other[d * slots + j], col_refs[d][lag, j : j + 1, :], 0.0
                    )
            out_ref[lag] = total.astype(jnp.bfloat16)

    return pl.pallas_call(
        kernel,
        out_shape=jax.ShapeDtypeStruct((LAGS, blk_dev, block_size), jnp.bfloat16),
        in_specs=[SMEM, SMEM] + [VMEM] * (2 * groups),
        out_specs=VMEM,
        compiler_params=PARAMS,
        cost_estimate=cost(0.8),
    )(first_of, served, *rows, *cols)


def local(readings, present, pair_first, pair_second):
    blk_dev, block_size, steps_here = readings.shape
    pair_count = pair_first.shape[0]
    sensor_count = lax.axis_size("sensor")
    tm_count = lax.axis_size("tm")
    lag_count = lax.axis_size("lag")
    home = lax.axis_index("sensor")
    tm_place = lax.axis_index("tm")
    lag_place = lax.axis_index("lag")
    per_row = block_size // (tm_count * lag_count)
    groups = sorted({d % sensor_count for d in range(-REACH, REACH + 1)})
    slot_count = len(groups) * CAP

    first_index = pair_first - home * blk_dev
    owner = pair_second // blk_dev
    partner_index = pair_second - owner * blk_dev
    positions = jnp.arange(pair_count)
    earlier = (owner[:, None] == owner[None, :]) & (positions[None, :] < positions[:, None])
    rank = jnp.sum(earlier.astype(jnp.int32), axis=1)
    distance = (owner - home + sensor_count) % sensor_count
    group = jnp.sum(
        jnp.where(distance[:, None] == jnp.array(groups)[None, :], jnp.arange(len(groups)), 0),
        axis=1,
    )
    slot = group * CAP + (lag_place - rank + CAP) % CAP
    hot = slot[:, None] == jnp.arange(slot_count)[None, :]
    requests = jnp.sum(jnp.where(hot, partner_index[:, None], 0), axis=0)
    pair_of = jnp.sum(jnp.where(hot, positions[:, None] + 1, 0), axis=0) - 1
    first_of = jnp.sum(jnp.where(hot, first_index[:, None], 0), axis=0)

    served = [requests[:CAP]] + [
        rotated(requests[i * CAP : (i + 1) * CAP], "sensor", d)
        for i, d in enumerate(groups)
        if i > 0
    ]
    turns = jnp.arange(tm_count)
    row_starts = ((tm_place + turns) % tm_count * lag_count + lag_place) * per_row
    sent = pack_first(readings, present, first_index, row_starts, per_row)
    firsts = [sent[0]] + [rotated(sent[k], "tm", k) for k in range(1, tm_count)]
    places = jnp.concatenate([(tm_place - turns) % tm_count, row_starts[:1]])

    packed = pack_blocks(
        readings, present, jnp.concatenate([requests[:CAP]] + [s[:1] for s in served[1:]])
    )
    here, away = packed[:CAP], packed[CAP:]
    cov = None
    rows, cols = [], []
    for i, d in enumerate(groups):
        own = here[0] if i == 0 else rotated(away[i - 1], "sensor", -d)
        own_windows = [own] + [rotated(own, "tm", k) for k in range(1, tm_count)]
        blocks = [own_windows]
        for j in range(1, lag_count):
            blocks.append(
                [
                    here[j] if i == 0 and k == 0 else rotated(own_windows[k], "lag", j)
                    for k in range(tm_count)
                ]
            )
        cov, row, col = covariances(
            pair_of[i * CAP : (i + 1) * CAP],
            places,
            firsts,
            blocks,
            cov,
            pair_count,
            per_row,
            block_size,
        )
        rows.append(row)
        cols.append(col if i == 0 else rotated(col, "sensor", d))
    partial = fold(first_of, jnp.concatenate(served), rows, cols, blk_dev)
    partial = partial.astype(jnp.float32)
    if lag_count == 2:
        partial = partial + rotated(partial.astype(jnp.bfloat16), "lag", 1).astype(jnp.float32)
    else:
        partial = lax.psum(partial.astype(jnp.bfloat16), "lag").astype(jnp.float32)
    partial = partial.astype(jnp.bfloat16)
    if tm_count == 2:
        strength = partial.astype(jnp.float32) + rotated(partial, "tm", 1).astype(jnp.float32)
    else:
        strength = lax.psum(partial, "tm").astype(jnp.float32)
    return (cov, strength)


def solution(mesh):
    in_specs = (
        P(("parts", "sensor"), None, "tm"),
        P(("parts", "sensor"), "tm"),
        P(("parts", "sensor")),
        P(("parts", "sensor")),
    )
    out_specs = (
        P(("parts", "sensor"), None, ("tm", "lag"), None),
        P(None, ("parts", "sensor"), None),
    )
    return jax.shard_map(local, mesh=mesh, in_specs=in_specs, out_specs=out_specs, check_vma=False)
```

```python
import jax
import jax.numpy as jnp
import numpy as np
from jax import lax
from jax.experimental import pallas as pl
from jax.experimental.pallas import tpu as pltpu
from jax.sharding import PartitionSpec as P

LAGS = 25
REACH = 3
CAP = 2
PAD = 16
MASK_ROWS = 8
LAG_ROWS = 32
VMEM = pl.BlockSpec(memory_space=pltpu.VMEM)
SMEM = pl.BlockSpec(memory_space=pltpu.SMEM)
ANY = pl.BlockSpec(memory_space=pl.ANY)
PEAK = 1.15e9
PARAMS = pltpu.CompilerParams(vmem_limit_bytes=24 * 1024 * 1024)
WIDE = pltpu.CompilerParams(vmem_limit_bytes=55_000_000)


def cost(microseconds):
    return pl.CostEstimate(
        flops=int(microseconds * PEAK), bytes_accessed=1024, transcendentals=0
    )


def rotated(block, axis, distance):
    size = lax.axis_size(axis)
    return lax.ppermute(block, axis, [(i, (i + distance) % size) for i in range(size)])


def mask_rows(present_ref, index, rows):
    row = present_ref[pl.ds(index, 1), :].astype(jnp.float32)
    return jnp.broadcast_to(row, (rows, row.shape[1]))


def pack_blocks(readings, present, indices):
    _, rows, steps = readings.shape
    count = indices.shape[0]

    def kernel(index_ref, readings_ref, present_hbm, *rest):
        outs, sems, present_ref, present_sem = rest[:count], *rest[count:]
        masks = pltpu.make_async_copy(present_hbm, present_ref, present_sem)
        masks.start()
        copies = [
            pltpu.make_async_copy(
                readings_ref.at[index_ref[i]], outs[i].at[pl.ds(0, rows)], sems.at[i]
            )
            for i in range(count)
        ]
        for copy in copies:
            copy.start()
        masks.wait()
        for i in range(count):
            outs[i][rows : rows + MASK_ROWS, :] = mask_rows(
                present_ref, index_ref[i], MASK_ROWS
            ).astype(jnp.bfloat16)
        for copy in copies:
            copy.wait()

    return pl.pallas_call(
        kernel,
        out_shape=[jax.ShapeDtypeStruct((rows + MASK_ROWS, steps), jnp.bfloat16)] * count,
        in_specs=[SMEM, ANY, ANY],
        out_specs=[VMEM] * count,
        scratch_shapes=[
            pltpu.SemaphoreType.DMA((count,)),
            pltpu.VMEM(present.shape, present.dtype),
            pltpu.SemaphoreType.DMA,
        ],
        compiler_params=WIDE,
        cost_estimate=cost(1.0),
    )(indices, readings, present)


def pack_first(readings, present, first_index, row_starts, per_row):
    _, _, steps = readings.shape
    pairs = first_index.shape[0]
    count = row_starts.shape[0]

    def kernel(first_ref, start_ref, readings_ref, present_hbm, *rest):
        outs, sems, present_ref, present_sem = rest[:count], *rest[count:]
        masks_copy = pltpu.make_async_copy(present_hbm, present_ref, present_sem)
        masks_copy.start()
        copies = []
        for k in range(count):
            start = pl.multiple_of(start_ref[k], per_row)
            for p in range(pairs):
                copies.append(
                    pltpu.make_async_copy(
                        readings_ref.at[first_ref[p], pl.ds(start, per_row)],
                        outs[k].at[pl.ds(p * per_row, per_row)],
                        sems.at[k, p],
                    )
                )
        for copy in copies:
            copy.start()
        masks_copy.wait()
        rows = lax.broadcasted_iota(jnp.int32, (PAD, steps), 0)
        masks = jnp.zeros((PAD, steps), jnp.float32)
        for p in range(pairs):
            masks = jnp.where(rows == p, mask_rows(present_ref, first_ref[p], PAD), masks)
        for k in range(count):
            outs[k][pairs * per_row : pairs * per_row + PAD, :] = masks.astype(jnp.bfloat16)
        for copy in copies:
            copy.wait()

    return pl.pallas_call(
        kernel,
        out_shape=[jax.ShapeDtypeStruct((pairs * per_row + PAD, steps), jnp.bfloat16)] * count,
        in_specs=[SMEM, SMEM, ANY, ANY],
        out_specs=[VMEM] * count,
        scratch_shapes=[
            pltpu.SemaphoreType.DMA((count, pairs)),
            pltpu.VMEM(present.shape, present.dtype),
            pltpu.SemaphoreType.DMA,
        ],
        compiler_params=WIDE,
        cost_estimate=cost(1.4),
    )(first_index, row_starts, readings, present)


def centered_windows(raw, masks):
    total = sum(jnp.sum(r * m, axis=1, keepdims=True) for r, m in zip(raw, masks))
    count = sum(jnp.sum(m, axis=1, keepdims=True) for m in masks)
    average = total / count
    return [(r - average) * m for r, m in zip(raw, masks)]


def covariances(pair_of, places, firsts, blocks, carried, pairs, per_row, block_size):
    windows = len(firsts)
    slots = len(blocks)
    steps = firsts[0].shape[1]
    total_steps = windows * steps
    shifts = (LAGS + 1) // 2
    scales = 1.0 / np.sqrt(np.float32(total_steps) - np.arange(LAGS, dtype=np.float32))
    quarter = 128 // per_row
    flat = [block for slot in blocks for block in slot]

    def kernel(pair_ref, place_ref, *rest):
        first_refs = rest[:windows]
        block_refs = rest[windows : windows + slots * windows]
        rest = rest[windows + slots * windows + (carried is not None) :]
        cov_ref, row_ref, col_ref, left, right, product, squares, ready, first_part, sems = rest

        def prepare(j):
            pair = jnp.maximum(pair_ref[j], 0)
            base = pl.multiple_of(pair * per_row, per_row)
            which = lax.broadcasted_iota(jnp.int32, (PAD, steps), 0) == pair
            raw, masks = [], []
            for k in range(windows):
                raw.append(first_refs[k][pl.ds(base, per_row), :].astype(jnp.float32))
                all_masks = first_refs[k][pairs * per_row : pairs * per_row + PAD, :]
                masks.append(
                    jnp.sum(
                        jnp.where(which, all_masks.astype(jnp.float32), 0.0), axis=0, keepdims=True
                    )
                )
            for k, part in enumerate(centered_windows(raw, masks)):
                at = pl.multiple_of(place_ref[k] * steps, steps)
                first_part[j, :, pl.ds(at, steps)] = part
            raw, masks = [], []
            for k in range(windows):
                ref = block_refs[j * windows + k]
                raw.append(ref[0:block_size, :].astype(jnp.float32))
                masks.append(ref[block_size : block_size + 1, :].astype(jnp.float32))
            for k, part in enumerate(centered_windows(raw, masks)):
                at = pl.multiple_of(place_ref[k] * steps, steps)
                right[j, 0:block_size, pl.ds(at, steps)] = part.astype(jnp.bfloat16)
            whole = right[j, 0:block_size, :].astype(jnp.float32)
            lane = lax.broadcasted_iota(jnp.int32, whole.shape, 1)
            moved = pltpu.roll(whole, total_steps - 1, 1)
            right[j, block_size : 2 * block_size, :] = jnp.where(
                lane < total_steps - 1, moved, 0.0
            ).astype(jnp.bfloat16)
            whole = first_part[j]
            lane = lax.broadcasted_iota(jnp.int32, whole.shape, 1)
            for m in range(shifts):
                moved = whole if m == 0 else pltpu.roll(whole, 2 * m, 1)
                left[j, m * per_row : (m + 1) * per_row, :] = jnp.where(
                    lane >= 2 * m, moved, 0.0
                ).astype(jnp.bfloat16)

        def multiply(j):
            product[j] = lax.dot_general(
                left[j], right[j], (((1,), (1,)), ((), ())), preferred_element_type=jnp.float32
            )

        def finish(j):
            def standard(lag):
                m, odd = lag // 2, lag % 2
                return product[
                    j,
                    m * per_row : (m + 1) * per_row,
                    odd * block_size : (odd + 1) * block_size,
                ] * float(scales[lag])

            for lag in range(LAGS):
                ready[j, lag] = standard(lag).astype(jnp.bfloat16)

            @pl.when(pair_ref[j] >= 0)
            def _():
                pltpu.make_async_copy(ready.at[j], cov_ref.at[pair_ref[j]], sems.at[j]).start()

            used = jnp.where(pair_ref[j] >= 0, 1.0 / block_size, 0.0)
            for lag in range(LAGS):
                square = standard(lag)
                square = square * square
                col_ref[lag, j : j + 1, :] = jnp.sum(square, axis=0, keepdims=True) * used
                squares[j, lag * per_row : (lag + 1) * per_row, :] = square.astype(jnp.bfloat16)
            ones = jnp.full((8, block_size), 1.0 / block_size, jnp.bfloat16)
            sums = lax.dot_general(
                ones, squares[j], (((1,), (1,)), ((), ())), preferred_element_type=jnp.float32
            )
            start = place_ref[windows]
            lane = lax.broadcasted_iota(jnp.int32, (8, 128), 1)
            level = lax.broadcasted_iota(jnp.int32, (8, 128), 0)
            mine = (lane >= start) & (lane < start + per_row) & (pair_ref[j] >= 0)
            tiles = [jnp.zeros((8, 128), jnp.float32) for _ in range(LAG_ROWS // 8)]
            for lag in range(LAGS):
                q, r = lag // quarter, lag % quarter
                piece = sums[:, q * 128 : (q + 1) * 128]
                piece = pltpu.roll(piece, lax.rem(start + 128 - r * per_row, 128), 1)
                tiles[lag // 8] = jnp.where(mine & (level == lag % 8), piece, tiles[lag // 8])
            for i, tile in enumerate(tiles):
                row_ref[j, i * 8 : (i + 1) * 8, :] = tile

        for j in range(slots):
            prepare(j)
        for j in range(slots):
            multiply(j)
        for j in range(slots):
            finish(j)
        for j in range(slots):

            @pl.when(pair_ref[j] >= 0)
            def _():
                pltpu.make_async_copy(ready.at[j], cov_ref.at[pair_ref[j]], sems.at[j]).wait()

    operands = [pair_of, places, *firsts, *flat]
    specs = [SMEM, SMEM] + [VMEM] * (len(firsts) + len(flat))
    aliases = {}
    if carried is not None:
        aliases = {len(operands): 0}
        operands.append(carried)
        specs.append(ANY)
    wide = -(-LAGS * per_row // 128) * 128
    return pl.pallas_call(
        kernel,
        out_shape=[
            jax.ShapeDtypeStruct((pairs, LAGS, per_row, block_size), jnp.bfloat16),
            jax.ShapeDtypeStruct((slots, LAG_ROWS, block_size), jnp.float32),
            jax.ShapeDtypeStruct((LAGS, slots, block_size), jnp.float32),
        ],
        in_specs=specs,
        out_specs=[ANY, VMEM, VMEM],
        scratch_shapes=[
            pltpu.VMEM((slots, shifts * per_row, total_steps), jnp.bfloat16),
            pltpu.VMEM((slots, 2 * block_size, total_steps), jnp.bfloat16),
            pltpu.VMEM((slots, shifts * per_row, 2 * block_size), jnp.float32),
            pltpu.VMEM((slots, wide, block_size), jnp.bfloat16),
            pltpu.VMEM((slots, LAGS, per_row, block_size), jnp.bfloat16),
            pltpu.VMEM((slots, per_row, total_steps), jnp.float32),
            pltpu.SemaphoreType.DMA((slots,)),
        ],
        input_output_aliases=aliases,
        compiler_params=PARAMS,
        cost_estimate=cost(1.5 * slots),
    )(*operands)


def fold(first_of, served, rows, cols, blk_dev):
    groups = len(rows)
    slots, _, block_size = rows[0].shape

    def kernel(first_ref, served_ref, *rest):
        row_refs, col_refs, out_ref = rest[:groups], rest[groups : 2 * groups], rest[2 * groups]
        place = lax.broadcasted_iota(jnp.int32, (blk_dev, block_size), 0)
        own, other = [], []
        for d in range(groups):
            for j in range(slots):
                own.append(place == first_ref[d * slots + j])
                other.append(place == served_ref[d * slots + j])
        for lag in range(LAGS):
            total = jnp.zeros((blk_dev, block_size), jnp.float32)
            for d in range(groups):
                for j in range(slots):
                    total = total + jnp.where(
                        own[d * slots + j], row_refs[d][j, lag : lag + 1, :], 0.0
                    )
                    total = total + jnp.where(
                        other[d * slots + j], col_refs[d][lag, j : j + 1, :], 0.0
                    )
            out_ref[lag] = total.astype(jnp.bfloat16)

    return pl.pallas_call(
        kernel,
        out_shape=jax.ShapeDtypeStruct((LAGS, blk_dev, block_size), jnp.bfloat16),
        in_specs=[SMEM, SMEM] + [VMEM] * (2 * groups),
        out_specs=VMEM,
        compiler_params=PARAMS,
        cost_estimate=cost(0.8),
    )(first_of, served, *rows, *cols)


def local(readings, present, pair_first, pair_second):
    blk_dev, block_size, steps_here = readings.shape
    pair_count = pair_first.shape[0]
    sensor_count = lax.axis_size("sensor")
    tm_count = lax.axis_size("tm")
    lag_count = lax.axis_size("lag")
    home = lax.axis_index("sensor")
    tm_place = lax.axis_index("tm")
    lag_place = lax.axis_index("lag")
    per_row = block_size // (tm_count * lag_count)
    groups = sorted({d % sensor_count for d in range(-REACH, REACH + 1)})
    slot_count = len(groups) * CAP

    first_index = pair_first - home * blk_dev
    owner = pair_second // blk_dev
    partner_index = pair_second - owner * blk_dev
    positions = jnp.arange(pair_count)
    earlier = (owner[:, None] == owner[None, :]) & (positions[None, :] < positions[:, None])
    rank = jnp.sum(earlier.astype(jnp.int32), axis=1)
    distance = (owner - home + sensor_count) % sensor_count
    group = jnp.sum(
        jnp.where(distance[:, None] == jnp.array(groups)[None, :], jnp.arange(len(groups)), 0),
        axis=1,
    )
    slot = group * CAP + (lag_place - rank + CAP) % CAP
    hot = slot[:, None] == jnp.arange(slot_count)[None, :]
    requests = jnp.sum(jnp.where(hot, partner_index[:, None], 0), axis=0)
    pair_of = jnp.sum(jnp.where(hot, positions[:, None] + 1, 0), axis=0) - 1
    first_of = jnp.sum(jnp.where(hot, first_index[:, None], 0), axis=0)

    served = [requests[:CAP]] + [
        rotated(requests[i * CAP : (i + 1) * CAP], "sensor", d)
        for i, d in enumerate(groups)
        if i > 0
    ]
    turns = jnp.arange(tm_count)
    row_starts = ((tm_place + turns) % tm_count * lag_count + lag_place) * per_row
    sent = pack_first(readings, present, first_index, row_starts, per_row)
    firsts = [sent[0]] + [rotated(sent[k], "tm", k) for k in range(1, tm_count)]
    places = jnp.concatenate([(tm_place - turns) % tm_count, row_starts[:1]])

    packed = pack_blocks(
        readings, present, jnp.concatenate([requests[:CAP]] + [s[:1] for s in served[1:]])
    )
    here, away = list(packed[:CAP]), list(packed[CAP:])
    cov = None
    rows, cols = [], []
    for i, d in enumerate(groups):
        last = i == len(groups) - 1
        own = here[0] if i == 0 else rotated(away[i - 1], "sensor", -d)
        if last:
            own, rows[0] = lax.optimization_barrier((own, rows[0]))
        own_windows = [own] + [rotated(own, "tm", k) for k in range(1, tm_count)]
        if last:
            own_windows[-1], rows[-1] = lax.optimization_barrier((own_windows[-1], rows[-1]))
        blocks = [own_windows]
        for j in range(1, lag_count):
            blocks.append(
                [
                    here[j] if i == 0 and k == 0 else rotated(own_windows[k], "lag", j)
                    for k in range(tm_count)
                ]
            )
        cov, row, col = covariances(
            pair_of[i * CAP : (i + 1) * CAP],
            places,
            firsts,
            blocks,
            cov,
            pair_count,
            per_row,
            block_size,
        )
        rows.append(row)
        cols.append(col if i == 0 else rotated(col, "sensor", d))
    partial = fold(first_of, jnp.concatenate(served), rows, cols, blk_dev)
    partial = partial.astype(jnp.float32)
    if lag_count == 2:
        partial = partial + rotated(partial.astype(jnp.bfloat16), "lag", 1).astype(jnp.float32)
    else:
        partial = lax.psum(partial.astype(jnp.bfloat16), "lag").astype(jnp.float32)
    partial = partial.astype(jnp.bfloat16)
    if tm_count == 2:
        strength = partial.astype(jnp.float32) + rotated(partial, "tm", 1).astype(jnp.float32)
    else:
        strength = lax.psum(partial, "tm").astype(jnp.float32)
    return (cov, strength)


def solution(mesh):
    in_specs = (
        P(("parts", "sensor"), None, "tm"),
        P(("parts", "sensor"), "tm"),
        P(("parts", "sensor")),
        P(("parts", "sensor")),
    )
    out_specs = (
        P(("parts", "sensor"), None, ("tm", "lag"), None),
        P(None, ("parts", "sensor"), None),
    )
    return jax.shard_map(local, mesh=mesh, in_specs=in_specs, out_specs=out_specs, check_vma=False)
```

```python
import jax
import jax.numpy as jnp
import numpy as np
from jax import lax
from jax.experimental import pallas as pl
from jax.experimental.pallas import tpu as pltpu
from jax.sharding import PartitionSpec as P

LAGS = 25
REACH = 3
CAP = 2
PAD = 16
MASK_ROWS = 8
LAG_ROWS = 32
VMEM = pl.BlockSpec(memory_space=pltpu.VMEM)
SMEM = pl.BlockSpec(memory_space=pltpu.SMEM)
ANY = pl.BlockSpec(memory_space=pl.ANY)
PEAK = 1.15e9
PARAMS = pltpu.CompilerParams(vmem_limit_bytes=24 * 1024 * 1024)
WIDE = pltpu.CompilerParams(vmem_limit_bytes=55_000_000)


def cost(microseconds):
    return pl.CostEstimate(
        flops=int(microseconds * PEAK), bytes_accessed=1024, transcendentals=0
    )


def rotated(block, axis, distance):
    size = lax.axis_size(axis)
    return lax.ppermute(block, axis, [(i, (i + distance) % size) for i in range(size)])


def mask_rows(present_ref, index, rows):
    row = present_ref[pl.ds(index, 1), :].astype(jnp.float32)
    return jnp.broadcast_to(row, (rows, row.shape[1]))


def pack_blocks(readings, present, indices):
    _, rows, steps = readings.shape
    count = indices.shape[0]

    def kernel(index_ref, readings_ref, present_hbm, *rest):
        outs, sems, present_ref, present_sem = rest[:count], *rest[count:]
        masks = pltpu.make_async_copy(present_hbm, present_ref, present_sem)
        masks.start()
        copies = [
            pltpu.make_async_copy(
                readings_ref.at[index_ref[i]], outs[i].at[pl.ds(0, rows)], sems.at[i]
            )
            for i in range(count)
        ]
        for copy in copies:
            copy.start()
        masks.wait()
        for i in range(count):
            outs[i][rows : rows + MASK_ROWS, :] = mask_rows(
                present_ref, index_ref[i], MASK_ROWS
            ).astype(jnp.bfloat16)
        for copy in copies:
            copy.wait()

    return pl.pallas_call(
        kernel,
        out_shape=[jax.ShapeDtypeStruct((rows + MASK_ROWS, steps), jnp.bfloat16)] * count,
        in_specs=[SMEM, ANY, ANY],
        out_specs=[VMEM] * count,
        scratch_shapes=[
            pltpu.SemaphoreType.DMA((count,)),
            pltpu.VMEM(present.shape, present.dtype),
            pltpu.SemaphoreType.DMA,
        ],
        compiler_params=WIDE,
        cost_estimate=cost(1.0),
    )(indices, readings, present)


def pack_first(readings, present, first_index, row_starts, per_row):
    _, _, steps = readings.shape
    pairs = first_index.shape[0]
    count = row_starts.shape[0]

    def kernel(first_ref, start_ref, readings_ref, present_hbm, *rest):
        outs, sems, present_ref, present_sem = rest[:count], *rest[count:]
        masks_copy = pltpu.make_async_copy(present_hbm, present_ref, present_sem)
        masks_copy.start()
        copies = []
        for k in range(count):
            start = pl.multiple_of(start_ref[k], per_row)
            for p in range(pairs):
                copies.append(
                    pltpu.make_async_copy(
                        readings_ref.at[first_ref[p], pl.ds(start, per_row)],
                        outs[k].at[pl.ds(p * per_row, per_row)],
                        sems.at[k, p],
                    )
                )
        for copy in copies:
            copy.start()
        masks_copy.wait()
        rows = lax.broadcasted_iota(jnp.int32, (PAD, steps), 0)
        masks = jnp.zeros((PAD, steps), jnp.float32)
        for p in range(pairs):
            masks = jnp.where(rows == p, mask_rows(present_ref, first_ref[p], PAD), masks)
        for k in range(count):
            outs[k][pairs * per_row : pairs * per_row + PAD, :] = masks.astype(jnp.bfloat16)
        for copy in copies:
            copy.wait()

    return pl.pallas_call(
        kernel,
        out_shape=[jax.ShapeDtypeStruct((pairs * per_row + PAD, steps), jnp.bfloat16)] * count,
        in_specs=[SMEM, SMEM, ANY, ANY],
        out_specs=[VMEM] * count,
        scratch_shapes=[
            pltpu.SemaphoreType.DMA((count, pairs)),
            pltpu.VMEM(present.shape, present.dtype),
            pltpu.SemaphoreType.DMA,
        ],
        compiler_params=WIDE,
        cost_estimate=cost(1.4),
    )(first_index, row_starts, readings, present)


def centered_windows(raw, masks):
    total = sum(jnp.sum(r * m, axis=1, keepdims=True) for r, m in zip(raw, masks))
    count = sum(jnp.sum(m, axis=1, keepdims=True) for m in masks)
    average = total / count
    return [(r - average) * m for r, m in zip(raw, masks)]


def covariances(pair_of, places, firsts, blocks, carried, pairs, per_row, block_size):
    windows = len(firsts)
    slots = len(blocks)
    steps = firsts[0].shape[1]
    total_steps = windows * steps
    shifts = (LAGS + 1) // 2
    scales = 1.0 / np.sqrt(np.float32(total_steps) - np.arange(LAGS, dtype=np.float32))
    quarter = 128 // per_row
    flat = [block for slot in blocks for block in slot]

    def kernel(pair_ref, place_ref, *rest):
        first_refs = rest[:windows]
        block_refs = rest[windows : windows + slots * windows]
        rest = rest[windows + slots * windows + (carried is not None) :]
        cov_ref, row_ref, col_ref, left, right, product, squares, ready, first_part, sems = rest

        def prepare(j):
            pair = jnp.maximum(pair_ref[j], 0)
            base = pl.multiple_of(pair * per_row, per_row)
            which = lax.broadcasted_iota(jnp.int32, (PAD, steps), 0) == pair
            raw, masks = [], []
            for k in range(windows):
                raw.append(first_refs[k][pl.ds(base, per_row), :].astype(jnp.float32))
                all_masks = first_refs[k][pairs * per_row : pairs * per_row + PAD, :]
                masks.append(
                    jnp.sum(
                        jnp.where(which, all_masks.astype(jnp.float32), 0.0), axis=0, keepdims=True
                    )
                )
            for k, part in enumerate(centered_windows(raw, masks)):
                at = pl.multiple_of(place_ref[k] * steps, steps)
                first_part[j, :, pl.ds(at, steps)] = part
            raw, masks = [], []
            for k in range(windows):
                ref = block_refs[j * windows + k]
                raw.append(ref[0:block_size, :].astype(jnp.float32))
                masks.append(ref[block_size : block_size + 1, :].astype(jnp.float32))
            for k, part in enumerate(centered_windows(raw, masks)):
                at = pl.multiple_of(place_ref[k] * steps, steps)
                right[j, 0:block_size, pl.ds(at, steps)] = part.astype(jnp.bfloat16)
            whole = right[j, 0:block_size, :].astype(jnp.float32)
            lane = lax.broadcasted_iota(jnp.int32, whole.shape, 1)
            moved = pltpu.roll(whole, total_steps - 1, 1)
            right[j, block_size : 2 * block_size, :] = jnp.where(
                lane < total_steps - 1, moved, 0.0
            ).astype(jnp.bfloat16)
            whole = first_part[j]
            lane = lax.broadcasted_iota(jnp.int32, whole.shape, 1)
            for m in range(shifts):
                moved = whole if m == 0 else pltpu.roll(whole, 2 * m, 1)
                left[j, m * per_row : (m + 1) * per_row, :] = jnp.where(
                    lane >= 2 * m, moved, 0.0
                ).astype(jnp.bfloat16)

        def multiply(j):
            product[j] = lax.dot_general(
                left[j], right[j], (((1,), (1,)), ((), ())), preferred_element_type=jnp.float32
            )

        def standard(j, lag):
            m, odd = lag // 2, lag % 2
            return product[
                j,
                m * per_row : (m + 1) * per_row,
                odd * block_size : (odd + 1) * block_size,
            ] * float(scales[lag])

        def hand_over(j):
            for lag in range(LAGS):
                ready[j, lag] = standard(j, lag).astype(jnp.bfloat16)

            @pl.when(pair_ref[j] >= 0)
            def _():
                pltpu.make_async_copy(ready.at[j], cov_ref.at[pair_ref[j]], sems.at[j]).start()

        def finish(j):
            used = jnp.where(pair_ref[j] >= 0, 1.0 / block_size, 0.0)
            for lag in range(LAGS):
                square = standard(j, lag)
                square = square * square
                col_ref[lag, j : j + 1, :] = jnp.sum(square, axis=0, keepdims=True) * used
                squares[j, lag * per_row : (lag + 1) * per_row, :] = square.astype(jnp.bfloat16)
            ones = jnp.full((8, block_size), 1.0 / block_size, jnp.bfloat16)
            sums = lax.dot_general(
                ones, squares[j], (((1,), (1,)), ((), ())), preferred_element_type=jnp.float32
            )
            start = place_ref[windows]
            lane = lax.broadcasted_iota(jnp.int32, (8, 128), 1)
            level = lax.broadcasted_iota(jnp.int32, (8, 128), 0)
            mine = (lane >= start) & (lane < start + per_row) & (pair_ref[j] >= 0)
            tiles = [jnp.zeros((8, 128), jnp.float32) for _ in range(LAG_ROWS // 8)]
            for lag in range(LAGS):
                q, r = lag // quarter, lag % quarter
                piece = sums[:, q * 128 : (q + 1) * 128]
                piece = pltpu.roll(piece, lax.rem(start + 128 - r * per_row, 128), 1)
                tiles[lag // 8] = jnp.where(mine & (level == lag % 8), piece, tiles[lag // 8])
            for i, tile in enumerate(tiles):
                row_ref[j, i * 8 : (i + 1) * 8, :] = tile

        for j in range(slots):
            prepare(j)
        for j in range(slots):
            multiply(j)
        for j in range(slots):
            hand_over(j)
        for j in range(slots):
            finish(j)
        for j in range(slots):

            @pl.when(pair_ref[j] >= 0)
            def _():
                pltpu.make_async_copy(ready.at[j], cov_ref.at[pair_ref[j]], sems.at[j]).wait()

    operands = [pair_of, places, *firsts, *flat]
    specs = [SMEM, SMEM] + [VMEM] * (len(firsts) + len(flat))
    aliases = {}
    if carried is not None:
        aliases = {len(operands): 0}
        operands.append(carried)
        specs.append(ANY)
    wide = -(-LAGS * per_row // 128) * 128
    return pl.pallas_call(
        kernel,
        out_shape=[
            jax.ShapeDtypeStruct((pairs, LAGS, per_row, block_size), jnp.bfloat16),
            jax.ShapeDtypeStruct((slots, LAG_ROWS, block_size), jnp.float32),
            jax.ShapeDtypeStruct((LAGS, slots, block_size), jnp.float32),
        ],
        in_specs=specs,
        out_specs=[ANY, VMEM, VMEM],
        scratch_shapes=[
            pltpu.VMEM((slots, shifts * per_row, total_steps), jnp.bfloat16),
            pltpu.VMEM((slots, 2 * block_size, total_steps), jnp.bfloat16),
            pltpu.VMEM((slots, shifts * per_row, 2 * block_size), jnp.float32),
            pltpu.VMEM((slots, wide, block_size), jnp.bfloat16),
            pltpu.VMEM((slots, LAGS, per_row, block_size), jnp.bfloat16),
            pltpu.VMEM((slots, per_row, total_steps), jnp.float32),
            pltpu.SemaphoreType.DMA((slots,)),
        ],
        input_output_aliases=aliases,
        compiler_params=PARAMS,
        cost_estimate=cost(1.5 * slots),
    )(*operands)


def fold(first_of, served, rows, cols, blk_dev):
    groups = len(rows)
    slots, _, block_size = rows[0].shape

    def kernel(first_ref, served_ref, *rest):
        row_refs, col_refs, out_ref = rest[:groups], rest[groups : 2 * groups], rest[2 * groups]
        place = lax.broadcasted_iota(jnp.int32, (blk_dev, block_size), 0)
        own, other = [], []
        for d in range(groups):
            for j in range(slots):
                own.append(place == first_ref[d * slots + j])
                other.append(place == served_ref[d * slots + j])
        for lag in range(LAGS):
            total = jnp.zeros((blk_dev, block_size), jnp.float32)
            for d in range(groups):
                for j in range(slots):
                    total = total + jnp.where(
                        own[d * slots + j], row_refs[d][j, lag : lag + 1, :], 0.0
                    )
                    total = total + jnp.where(
                        other[d * slots + j], col_refs[d][lag, j : j + 1, :], 0.0
                    )
            out_ref[lag] = total.astype(jnp.bfloat16)

    return pl.pallas_call(
        kernel,
        out_shape=jax.ShapeDtypeStruct((LAGS, blk_dev, block_size), jnp.bfloat16),
        in_specs=[SMEM, SMEM] + [VMEM] * (2 * groups),
        out_specs=VMEM,
        compiler_params=PARAMS,
        cost_estimate=cost(0.8),
    )(first_of, served, *rows, *cols)


def local(readings, present, pair_first, pair_second):
    blk_dev, block_size, steps_here = readings.shape
    pair_count = pair_first.shape[0]
    sensor_count = lax.axis_size("sensor")
    tm_count = lax.axis_size("tm")
    lag_count = lax.axis_size("lag")
    home = lax.axis_index("sensor")
    tm_place = lax.axis_index("tm")
    lag_place = lax.axis_index("lag")
    per_row = block_size // (tm_count * lag_count)
    groups = sorted({d % sensor_count for d in range(-REACH, REACH + 1)})
    slot_count = len(groups) * CAP

    both = lax.optimization_barrier(jnp.concatenate([pair_first, pair_second]))
    pair_first, pair_second = both[:pair_count], both[pair_count:]
    first_index = pair_first - home * blk_dev
    owner = pair_second // blk_dev
    partner_index = pair_second - owner * blk_dev
    positions = jnp.arange(pair_count)
    earlier = (owner[:, None] == owner[None, :]) & (positions[None, :] < positions[:, None])
    rank = jnp.sum(earlier.astype(jnp.int32), axis=1)
    distance = (owner - home + sensor_count) % sensor_count
    group = jnp.sum(
        jnp.where(distance[:, None] == jnp.array(groups)[None, :], jnp.arange(len(groups)), 0),
        axis=1,
    )
    slot = group * CAP + (lag_place - rank + CAP) % CAP
    hot = slot[:, None] == jnp.arange(slot_count)[None, :]
    requests = jnp.sum(jnp.where(hot, partner_index[:, None], 0), axis=0)
    pair_of = jnp.sum(jnp.where(hot, positions[:, None] + 1, 0), axis=0) - 1
    first_of = jnp.sum(jnp.where(hot, first_index[:, None], 0), axis=0)

    served = [requests[:CAP]] + [
        rotated(requests[i * CAP : (i + 1) * CAP], "sensor", d)
        for i, d in enumerate(groups)
        if i > 0
    ]
    turns = jnp.arange(tm_count)
    row_starts = ((tm_place + turns) % tm_count * lag_count + lag_place) * per_row
    sent = pack_first(readings, present, first_index, row_starts, per_row)
    firsts = [sent[0]] + [rotated(sent[k], "tm", k) for k in range(1, tm_count)]
    places = jnp.concatenate([(tm_place - turns) % tm_count, row_starts[:1]])

    packed = pack_blocks(
        readings, present, jnp.concatenate([requests[:CAP]] + [s[:1] for s in served[1:]])
    )
    here, away = list(packed[:CAP]), list(packed[CAP:])
    cov = None
    rows, cols = [], []
    for i, d in enumerate(groups):
        last = i == len(groups) - 1
        own = here[0] if i == 0 else rotated(away[i - 1], "sensor", -d)
        if last:
            own, rows[0] = lax.optimization_barrier((own, rows[0]))
        own_windows = [own] + [rotated(own, "tm", k) for k in range(1, tm_count)]
        if last:
            own_windows[-1], rows[-1] = lax.optimization_barrier((own_windows[-1], rows[-1]))
        blocks = [own_windows]
        for j in range(1, lag_count):
            blocks.append(
                [
                    here[j] if i == 0 and k == 0 else rotated(own_windows[k], "lag", j)
                    for k in range(tm_count)
                ]
            )
        cov, row, col = covariances(
            pair_of[i * CAP : (i + 1) * CAP],
            places,
            firsts,
            blocks,
            cov,
            pair_count,
            per_row,
            block_size,
        )
        rows.append(row)
        cols.append(col if i == 0 else rotated(col, "sensor", d))
    partial = fold(first_of, jnp.concatenate(served), rows, cols, blk_dev)
    partial = partial.astype(jnp.float32)
    if lag_count == 2:
        partial = partial + rotated(partial.astype(jnp.bfloat16), "lag", 1).astype(jnp.float32)
    else:
        partial = lax.psum(partial.astype(jnp.bfloat16), "lag").astype(jnp.float32)
    partial = partial.astype(jnp.bfloat16)
    if tm_count == 2:
        strength = partial.astype(jnp.float32) + rotated(partial, "tm", 1).astype(jnp.float32)
    else:
        strength = lax.psum(partial, "tm").astype(jnp.float32)
    return (cov, strength)


def solution(mesh):
    in_specs = (
        P(("parts", "sensor"), None, "tm"),
        P(("parts", "sensor"), "tm"),
        P(("parts", "sensor")),
        P(("parts", "sensor")),
    )
    out_specs = (
        P(("parts", "sensor"), None, ("tm", "lag"), None),
        P(None, ("parts", "sensor"), None),
    )
    return jax.shard_map(local, mesh=mesh, in_specs=in_specs, out_specs=out_specs, check_vma=False)
```

```python
import jax
import jax.numpy as jnp
import numpy as np
from jax import lax
from jax.experimental import pallas as pl
from jax.experimental.pallas import tpu as pltpu
from jax.sharding import PartitionSpec as P

LAGS = 25
REACH = 3
CAP = 2
PAD = 16
MASK_ROWS = 8
LAG_ROWS = 32
VMEM = pl.BlockSpec(memory_space=pltpu.VMEM)
SMEM = pl.BlockSpec(memory_space=pltpu.SMEM)
ANY = pl.BlockSpec(memory_space=pl.ANY)
PEAK = 1.15e9
PARAMS = pltpu.CompilerParams(vmem_limit_bytes=24 * 1024 * 1024)
WIDE = pltpu.CompilerParams(vmem_limit_bytes=55_000_000)


def cost(microseconds):
    return pl.CostEstimate(
        flops=int(microseconds * PEAK), bytes_accessed=1024, transcendentals=0
    )


def rotated(block, axis, distance):
    size = lax.axis_size(axis)
    return lax.ppermute(block, axis, [(i, (i + distance) % size) for i in range(size)])


def mask_rows(present_ref, index, rows):
    row = present_ref[pl.ds(index, 1), :].astype(jnp.float32)
    return jnp.broadcast_to(row, (rows, row.shape[1]))


def pack_blocks(readings, present, indices):
    _, rows, steps = readings.shape
    count = indices.shape[0]

    def kernel(index_ref, readings_ref, present_hbm, *rest):
        outs, sems, present_ref, present_sem = rest[:count], *rest[count:]
        masks = pltpu.make_async_copy(present_hbm, present_ref, present_sem)
        masks.start()
        copies = [
            pltpu.make_async_copy(
                readings_ref.at[index_ref[i]], outs[i].at[pl.ds(0, rows)], sems.at[i]
            )
            for i in range(count)
        ]
        for copy in copies:
            copy.start()
        masks.wait()
        for i in range(count):
            outs[i][rows : rows + MASK_ROWS, :] = mask_rows(
                present_ref, index_ref[i], MASK_ROWS
            ).astype(jnp.bfloat16)
        for copy in copies:
            copy.wait()

    return pl.pallas_call(
        kernel,
        out_shape=[jax.ShapeDtypeStruct((rows + MASK_ROWS, steps), jnp.bfloat16)] * count,
        in_specs=[SMEM, ANY, ANY],
        out_specs=[VMEM] * count,
        scratch_shapes=[
            pltpu.SemaphoreType.DMA((count,)),
            pltpu.VMEM(present.shape, present.dtype),
            pltpu.SemaphoreType.DMA,
        ],
        compiler_params=WIDE,
        cost_estimate=cost(1.0),
    )(indices, readings, present)


def pack_first(readings, present, first_index, row_starts, per_row):
    _, _, steps = readings.shape
    pairs = first_index.shape[0]
    count = row_starts.shape[0]

    def kernel(first_ref, start_ref, readings_ref, present_hbm, *rest):
        outs, sems, present_ref, present_sem = rest[:count], *rest[count:]
        masks_copy = pltpu.make_async_copy(present_hbm, present_ref, present_sem)
        masks_copy.start()
        copies = []
        for k in range(count):
            start = pl.multiple_of(start_ref[k], per_row)
            for p in range(pairs):
                copies.append(
                    pltpu.make_async_copy(
                        readings_ref.at[first_ref[p], pl.ds(start, per_row)],
                        outs[k].at[pl.ds(p * per_row, per_row)],
                        sems.at[k, p],
                    )
                )
        for copy in copies:
            copy.start()
        masks_copy.wait()
        rows = lax.broadcasted_iota(jnp.int32, (PAD, steps), 0)
        masks = jnp.zeros((PAD, steps), jnp.float32)
        for p in range(pairs):
            masks = jnp.where(rows == p, mask_rows(present_ref, first_ref[p], PAD), masks)
        for k in range(count):
            outs[k][pairs * per_row : pairs * per_row + PAD, :] = masks.astype(jnp.bfloat16)
        for copy in copies:
            copy.wait()

    return pl.pallas_call(
        kernel,
        out_shape=[jax.ShapeDtypeStruct((pairs * per_row + PAD, steps), jnp.bfloat16)] * count,
        in_specs=[SMEM, SMEM, ANY, ANY],
        out_specs=[VMEM] * count,
        scratch_shapes=[
            pltpu.SemaphoreType.DMA((count, pairs)),
            pltpu.VMEM(present.shape, present.dtype),
            pltpu.SemaphoreType.DMA,
        ],
        compiler_params=WIDE,
        cost_estimate=cost(1.4),
    )(first_index, row_starts, readings, present)


def centered_windows(raw, masks):
    total = sum(jnp.sum(r * m, axis=1, keepdims=True) for r, m in zip(raw, masks))
    count = sum(jnp.sum(m, axis=1, keepdims=True) for m in masks)
    average = total / count
    return [(r - average) * m for r, m in zip(raw, masks)]


def covariances(pair_of, places, firsts, blocks, carried, pairs, per_row, block_size):
    windows = len(firsts)
    slots = len(blocks)
    steps = firsts[0].shape[1]
    total_steps = windows * steps
    shifts = (LAGS + 1) // 2
    scales = 1.0 / np.sqrt(np.float32(total_steps) - np.arange(LAGS, dtype=np.float32))
    quarter = 128 // per_row
    flat = [block for slot in blocks for block in slot]

    def kernel(pair_ref, place_ref, *rest):
        first_refs = rest[:windows]
        block_refs = rest[windows : windows + slots * windows]
        rest = rest[windows + slots * windows + (carried is not None) :]
        cov_ref, row_ref, col_ref, left, right, product, squares, ready, first_part, sems = rest

        def prepare(j):
            pair = jnp.maximum(pair_ref[j], 0)
            base = pl.multiple_of(pair * per_row, per_row)
            which = lax.broadcasted_iota(jnp.int32, (PAD, steps), 0) == pair
            raw, masks = [], []
            for k in range(windows):
                raw.append(first_refs[k][pl.ds(base, per_row), :].astype(jnp.float32))
                all_masks = first_refs[k][pairs * per_row : pairs * per_row + PAD, :]
                masks.append(
                    jnp.sum(
                        jnp.where(which, all_masks.astype(jnp.float32), 0.0), axis=0, keepdims=True
                    )
                )
            for k, part in enumerate(centered_windows(raw, masks)):
                at = pl.multiple_of(place_ref[k] * steps, steps)
                first_part[j, :, pl.ds(at, steps)] = part
            raw, masks = [], []
            for k in range(windows):
                ref = block_refs[j * windows + k]
                raw.append(ref[0:block_size, :].astype(jnp.float32))
                masks.append(ref[block_size : block_size + 1, :].astype(jnp.float32))
            for k, part in enumerate(centered_windows(raw, masks)):
                at = pl.multiple_of(place_ref[k] * steps, steps)
                right[j, 0:block_size, pl.ds(at, steps)] = part.astype(jnp.bfloat16)
            whole = right[j, 0:block_size, :].astype(jnp.float32)
            lane = lax.broadcasted_iota(jnp.int32, whole.shape, 1)
            moved = pltpu.roll(whole, total_steps - 1, 1)
            right[j, block_size : 2 * block_size, :] = jnp.where(
                lane < total_steps - 1, moved, 0.0
            ).astype(jnp.bfloat16)
            whole = first_part[j]
            lane = lax.broadcasted_iota(jnp.int32, whole.shape, 1)
            for m in range(shifts):
                moved = whole if m == 0 else pltpu.roll(whole, 2 * m, 1)
                left[j, m * per_row : (m + 1) * per_row, :] = jnp.where(
                    lane >= 2 * m, moved, 0.0
                ).astype(jnp.bfloat16)

        def multiply(j):
            product[j] = lax.dot_general(
                left[j], right[j], (((1,), (1,)), ((), ())), preferred_element_type=jnp.float32
            )

        def standard(j, lag):
            m, odd = lag // 2, lag % 2
            return product[
                j,
                m * per_row : (m + 1) * per_row,
                odd * block_size : (odd + 1) * block_size,
            ] * float(scales[lag])

        def hand_over(j):
            for lag in range(LAGS):
                ready[j, lag] = standard(j, lag).astype(jnp.bfloat16)

            @pl.when(pair_ref[j] >= 0)
            def _():
                pltpu.make_async_copy(ready.at[j], cov_ref.at[pair_ref[j]], sems.at[j]).start()

        def finish(j):
            used = jnp.where(pair_ref[j] >= 0, 1.0 / block_size, 0.0)
            for lag in range(LAGS):
                square = standard(j, lag)
                square = square * square
                col_ref[lag, j : j + 1, :] = jnp.sum(square, axis=0, keepdims=True) * used
                squares[j, lag * per_row : (lag + 1) * per_row, :] = square.astype(jnp.bfloat16)
            ones = jnp.full((8, block_size), 1.0 / block_size, jnp.bfloat16)
            sums = lax.dot_general(
                ones, squares[j], (((1,), (1,)), ((), ())), preferred_element_type=jnp.float32
            )
            start = place_ref[windows]
            lane = lax.broadcasted_iota(jnp.int32, (8, 128), 1)
            level = lax.broadcasted_iota(jnp.int32, (8, 128), 0)
            mine = (lane >= start) & (lane < start + per_row) & (pair_ref[j] >= 0)
            tiles = [jnp.zeros((8, 128), jnp.float32) for _ in range(LAG_ROWS // 8)]
            for lag in range(LAGS):
                q, r = lag // quarter, lag % quarter
                piece = sums[:, q * 128 : (q + 1) * 128]
                piece = pltpu.roll(piece, lax.rem(start + 128 - r * per_row, 128), 1)
                tiles[lag // 8] = jnp.where(mine & (level == lag % 8), piece, tiles[lag // 8])
            for i, tile in enumerate(tiles):
                row_ref[j, i * 8 : (i + 1) * 8, :] = tile

        for j in range(slots):
            prepare(j)
        for j in range(slots):
            multiply(j)
        for j in range(slots):
            hand_over(j)
        for j in range(slots):
            finish(j)
        for j in range(slots):

            @pl.when(pair_ref[j] >= 0)
            def _():
                pltpu.make_async_copy(ready.at[j], cov_ref.at[pair_ref[j]], sems.at[j]).wait()

    operands = [pair_of, places, *firsts, *flat]
    specs = [SMEM, SMEM] + [VMEM] * (len(firsts) + len(flat))
    aliases = {}
    if carried is not None:
        aliases = {len(operands): 0}
        operands.append(carried)
        specs.append(ANY)
    wide = -(-LAGS * per_row // 128) * 128
    return pl.pallas_call(
        kernel,
        out_shape=[
            jax.ShapeDtypeStruct((pairs, LAGS, per_row, block_size), jnp.bfloat16),
            jax.ShapeDtypeStruct((slots, LAG_ROWS, block_size), jnp.float32),
            jax.ShapeDtypeStruct((LAGS, slots, block_size), jnp.float32),
        ],
        in_specs=specs,
        out_specs=[ANY, VMEM, VMEM],
        scratch_shapes=[
            pltpu.VMEM((slots, shifts * per_row, total_steps), jnp.bfloat16),
            pltpu.VMEM((slots, 2 * block_size, total_steps), jnp.bfloat16),
            pltpu.VMEM((slots, shifts * per_row, 2 * block_size), jnp.float32),
            pltpu.VMEM((slots, wide, block_size), jnp.bfloat16),
            pltpu.VMEM((slots, LAGS, per_row, block_size), jnp.bfloat16),
            pltpu.VMEM((slots, per_row, total_steps), jnp.float32),
            pltpu.SemaphoreType.DMA((slots,)),
        ],
        input_output_aliases=aliases,
        compiler_params=PARAMS,
        cost_estimate=cost(1.5 * slots),
    )(*operands)


def fold(first_of, served, rows, cols, blk_dev):
    groups = len(rows)
    slots, _, block_size = rows[0].shape

    def kernel(first_ref, served_ref, *rest):
        row_refs, col_refs, out_ref = rest[:groups], rest[groups : 2 * groups], rest[2 * groups]
        place = lax.broadcasted_iota(jnp.int32, (blk_dev, block_size), 0)
        own, other = [], []
        for d in range(groups):
            for j in range(slots):
                own.append(place == first_ref[d * slots + j])
                other.append(place == served_ref[d * slots + j])
        for lag in range(LAGS):
            total = jnp.zeros((blk_dev, block_size), jnp.float32)
            for d in range(groups):
                for j in range(slots):
                    total = total + jnp.where(
                        own[d * slots + j], row_refs[d][j, lag : lag + 1, :], 0.0
                    )
                    total = total + jnp.where(
                        other[d * slots + j], col_refs[d][lag, j : j + 1, :], 0.0
                    )
            out_ref[lag] = total.astype(jnp.bfloat16)

    return pl.pallas_call(
        kernel,
        out_shape=jax.ShapeDtypeStruct((LAGS, blk_dev, block_size), jnp.bfloat16),
        in_specs=[SMEM, SMEM] + [VMEM] * (2 * groups),
        out_specs=VMEM,
        compiler_params=PARAMS,
        cost_estimate=cost(0.8),
    )(first_of, served, *rows, *cols)


def local(readings, present, pair_first, pair_second):
    blk_dev, block_size, steps_here = readings.shape
    pair_count = pair_first.shape[0]
    sensor_count = lax.axis_size("sensor")
    tm_count = lax.axis_size("tm")
    lag_count = lax.axis_size("lag")
    home = lax.axis_index("sensor")
    tm_place = lax.axis_index("tm")
    lag_place = lax.axis_index("lag")
    per_row = block_size // (tm_count * lag_count)
    groups = sorted({d % sensor_count for d in range(-REACH, REACH + 1)})
    slot_count = len(groups) * CAP

    both = lax.optimization_barrier(jnp.concatenate([pair_first, pair_second]))
    pair_first, pair_second = both[:pair_count], both[pair_count:]
    first_index = pair_first - home * blk_dev
    owner = pair_second // blk_dev
    partner_index = pair_second - owner * blk_dev
    positions = jnp.arange(pair_count)
    earlier = (owner[:, None] == owner[None, :]) & (positions[None, :] < positions[:, None])
    rank = jnp.sum(earlier.astype(jnp.int32), axis=1)
    distance = (owner - home + sensor_count) % sensor_count
    group = jnp.sum(
        jnp.where(distance[:, None] == jnp.array(groups)[None, :], jnp.arange(len(groups)), 0),
        axis=1,
    )
    slot = group * CAP + (lag_place - rank + CAP) % CAP
    hot = slot[:, None] == jnp.arange(slot_count)[None, :]
    requests = jnp.sum(jnp.where(hot, partner_index[:, None], 0), axis=0)
    pair_of = jnp.sum(jnp.where(hot, positions[:, None] + 1, 0), axis=0) - 1
    first_of = jnp.sum(jnp.where(hot, first_index[:, None], 0), axis=0)

    served = [requests[:CAP]] + [
        rotated(requests[i * CAP : (i + 1) * CAP], "sensor", d)
        for i, d in enumerate(groups)
        if i > 0
    ]
    turns = jnp.arange(tm_count)
    row_starts = ((tm_place + turns) % tm_count * lag_count + lag_place) * per_row
    sent = pack_first(readings, present, first_index, row_starts, per_row)
    firsts = [sent[0]] + [rotated(sent[k], "tm", k) for k in range(1, tm_count)]
    places = jnp.concatenate([(tm_place - turns) % tm_count, row_starts[:1]])

    packed = pack_blocks(
        readings, present, jnp.concatenate([requests[:CAP]] + [s[:1] for s in served[1:]])
    )
    here, away = list(packed[:CAP]), list(packed[CAP:])
    cov = None
    rows, cols = [], []
    for i, d in enumerate(groups):
        last = i == len(groups) - 1
        own = here[0] if i == 0 else rotated(away[i - 1], "sensor", -d)
        if last:
            own, rows[0] = lax.optimization_barrier((own, rows[0]))
        own_windows = [own] + [rotated(own, "tm", k) for k in range(1, tm_count)]
        if last:
            own_windows[-1], rows[-1] = lax.optimization_barrier((own_windows[-1], rows[-1]))
        blocks = [own_windows]
        for j in range(1, lag_count):
            blocks.append(
                [
                    here[j] if i == 0 and k == 0 else rotated(own_windows[k], "lag", j)
                    for k in range(tm_count)
                ]
            )
        cov, row, col = covariances(
            pair_of[i * CAP : (i + 1) * CAP],
            places,
            firsts,
            blocks,
            cov,
            pair_count,
            per_row,
            block_size,
        )
        rows.append(row)
        cols.append(col if i == 0 else rotated(col, "sensor", d))
    partial = fold(first_of, jnp.concatenate(served), rows, cols, blk_dev)
    for axis, size in (("tm", tm_count), ("lag", lag_count)):
        if size == 2:
            other = rotated(partial.astype(jnp.bfloat16), axis, 1)
            partial = partial.astype(jnp.float32) + other.astype(jnp.float32)
        else:
            partial = lax.psum(partial.astype(jnp.bfloat16), axis)
        if axis == "tm":
            partial = partial.astype(jnp.bfloat16)
    strength = partial.astype(jnp.float32)
    return (cov, strength)


def solution(mesh):
    in_specs = (
        P(("parts", "sensor"), None, "tm"),
        P(("parts", "sensor"), "tm"),
        P(("parts", "sensor")),
        P(("parts", "sensor")),
    )
    out_specs = (
        P(("parts", "sensor"), None, ("tm", "lag"), None),
        P(None, ("parts", "sensor"), None),
    )
    return jax.shard_map(local, mesh=mesh, in_specs=in_specs, out_specs=out_specs, check_vma=False)
```
